32 devices in a mesh: fsdp: 16 (over z, y, x), seq: 2 (over core).
Axes of the slice: x: 2, y: 2, z: 4, core: 2. Of those that a mesh axis runs over, the one named last changes fastest.
Arguments:
- layer_input: bfloat16 [64, 1024, 576], P('fsdp', 'seq'), may hold values from -6 to 6
- segments: int32 [64, 1024], P('fsdp'), may hold values from 0 to 6, as said below
- project_weight: bfloat16 [552960], P(('fsdp', 'seq')), may hold values from -0.25 to 0.25
- output_weight: bfloat16 [331776], P(('fsdp', 'seq')), may hold values from -1 to 1
- gate_up_weight: bfloat16 [1769472], P(('fsdp', 'seq')), may hold values from -0.25 to 0.25
- down_weight: bfloat16 [884736], P(('fsdp', 'seq')), may hold values from -0.15625 to 0.15625
- gains: bfloat16 [1152], P('fsdp'), may hold values from 0.5 to 1.5
- cotangent: bfloat16 [64, 1024, 576], P('fsdp', 'seq'), may hold values from -6 to 6
Outputs:
- result: bfloat16 [64, 1024, 576], P('fsdp', 'seq')
- input_gradient: bfloat16 [64, 1024, 576], P('fsdp', 'seq')
- project_gradient: float32 [552960], P(('fsdp', 'seq'))
- output_gradient: float32 [331776], P(('fsdp', 'seq'))
- gate_up_gradient: float32 [1769472], P(('fsdp', 'seq'))
- down_gradient: float32 [884736], P(('fsdp', 'seq'))
- gains_gradient: float32 [1152], P('fsdp')
The draws below stay inside these ranges and needn't reach their ends.
Inputs may be any that keep to these rules, and one draw needn't show every extreme that they name: `segments`: in each sequence the segment numbers never fall, start at 0 and take each of the seven values 0 to 6; document 3 covers positions 256 through 3 * 256.
All inputs are finite; a program needn't handle non-finite values.
Results may differ from the reference program's by a relative error of at most 0.012.
Values may be sent and summed in bfloat16 or wider, within the bound.
A program may use at most 192 MiB of HBM per device.

```python
import math
import jax
import jax.numpy as jnp
from jax import lax

D = 576
H = 9
KV = 3
HD = 64
FF = 1536
LEN = 1024
NSEQ = 64


def draw_segments(key, part):
    key = jax.random.fold_in(key, 11)
    quarter = LEN // 4

    def one_row(row_key):
        first_key, second_key = jax.random.split(row_key)
        early = jax.random.permutation(first_key, quarter - 1)[:3] + 1
        later = jax.random.permutation(second_key, LEN - 3 * quarter - 1)[:3] + 3 * quarter + 1
        cuts = jnp.concatenate([early, later]).astype(jnp.int32)
        place = jnp.arange(LEN, dtype=jnp.int32)
        return jnp.sum((cuts[None, :] <= place[:, None]).astype(jnp.int32), axis=1)
    return jax.vmap(one_row)(jax.random.split(key, NSEQ))


def level_of(rng, dims, cuts, smallest, high):
    def one(axis_at, shards_of):
        heights = jax.random.uniform(jax.random.fold_in(jax.random.fold_in(rng, 6), axis_at), (shards_of,), jnp.float32, smallest / len(cuts), high / len(cuts))
        return jnp.repeat(jnp.exp(heights), dims[axis_at] // shards_of).reshape((-1,) + (1,) * (len(dims) - axis_at - 1))

    level = one(*cuts[0])
    for cut in cuts[1:]:
        level = level * one(*cut)
    return level


def noise(stream_key, dims, deviation, most, shards=(), held_as=jnp.bfloat16):
    result = jax.random.normal(stream_key, dims, jnp.float32) * deviation
    if len(shards) > 0:
        result = level_of(stream_key, dims, shards, -0.22, 0.18) * result
    return jnp.clip(result, min=-most, max=most).astype(held_as)


def setup_inputs(seed: int = 0) -> dict:
    key_list = jax.random.split(jax.random.key(seed), 9)
    return {
        "layer_input": noise(key_list[0], (NSEQ, LEN, D), 1.0, 6.0, ((0, 16), (1, 2))),
        "segments": draw_segments(jax.random.fold_in(key_list[8], 71), 0),
        "project_weight": noise(key_list[2], (D * (H + 2 * KV) * HD,), D ** -0.5, 0.25, ((0, 32),)),
        "output_weight": noise(key_list[3], (H * HD * D,), (H * HD // 16) ** -0.5, 1.0, ((0, 32),)),
        "gate_up_weight": noise(key_list[4], (2 * D * FF,), D ** -0.5, 0.25, ((0, 32),)),
        "down_weight": noise(key_list[5], (FF * D,), FF ** -0.5, 0.15625, ((0, 32),)),
        "gains": jnp.clip(1.0 + 0.1 * jax.random.normal(key_list[6], (2 * D,), jnp.float32), 0.5, 1.5).astype(jnp.bfloat16),
        "cotangent": noise(key_list[7], (NSEQ, LEN, D), 1.0, 6.0, ((0, 16), (1, 2))),
    }


FINEST_PRECISION = lax.Precision.HIGHEST
EPSILON = 1e-05
THETA = 100000.0
MASKED = -1e+30

@jax.custom_vjp
def low(v):
    return lax.optimization_barrier(v.astype(jnp.bfloat16)).astype(jnp.float32)

@jax.custom_vjp
def bfloat_backward(v):
    return v

def low_keep(v):
    return (low(v), None)

def low_pass(kept, grad):
    return (grad,)

def back_keep(v):
    return (v, None)

def back_low(kept, grad):
    return (low(grad),)
low.defvjp(low_keep, low_pass)
bfloat_backward.defvjp(back_keep, back_low)

def both_ways(value):
    return bfloat_backward(low(value))

def root_norm(values, gain):
    return values * lax.rsqrt(lax.optimization_barrier(jnp.mean(values * values, axis=-1, keepdims=True)) + EPSILON) * gain

def rotary_tables(positions, size):
    rates = THETA ** (-(jnp.arange(size // 2, dtype=jnp.float32) * 2.0) / size)
    angle = positions.astype(jnp.float32)[:, None] * rates[None, :]
    return (jnp.cos(angle), jnp.sin(angle))

def rotate(values, cosine, sine):
    middle = values.shape[-1] // 2
    first = values[..., :middle]
    second = values[..., middle:]
    cosine_row = cosine[:, None, :]
    sine_row = sine[:, None, :]
    return jnp.concatenate([first * cosine_row - second * sine_row, second * cosine_row + first * sine_row], axis=-1)

def attend(item):
    queries, keys, values, labels = item
    length = queries.shape[0]
    grouped = queries.reshape(length, KV, H // KV, HD)
    scores = jnp.einsum('tkgd,skd->kgts', grouped, keys, precision=FINEST_PRECISION) * HD ** (-0.5)
    scores = bfloat_backward(scores)
    place = jnp.arange(length)
    allowed = (place[None, :] <= place[:, None]) & (labels[None, :] == labels[:, None])
    scores = jnp.where(allowed, scores, MASKED)
    top = lax.optimization_barrier(jnp.max(scores, axis=-1, keepdims=True))
    powers = jnp.exp(scores - top)
    weights = low(powers / lax.optimization_barrier(jnp.sum(powers, axis=-1, keepdims=True)))
    attention_mixed = jnp.einsum('kgts,skd->tkgd', weights, values, precision=FINEST_PRECISION)
    return attention_mixed.reshape(length, H * HD)

def layer(hidden_features, attention_project_matrix, output_projection_matrix, gate_up_matrix, down_projection_matrix, gain_all, labels):
    count, length = (hidden_features.shape[0], hidden_features.shape[1])
    normalized_input = low(root_norm(hidden_features, gain_all[:D]))
    projected_rows = bfloat_backward(jnp.einsum('fwq,qa->fwa', normalized_input, attention_project_matrix, precision=FINEST_PRECISION))
    cosine, sine = rotary_tables(jnp.arange(length), HD)
    queries = low(rotate(projected_rows[..., :H * HD].reshape(count, length, H, HD), cosine, sine))
    keys = low(rotate(projected_rows[..., H * HD:(H + KV) * HD].reshape(count, length, KV, HD), cosine, sine))
    values = low(projected_rows[..., (H + KV) * HD:].reshape(count, length, KV, HD))
    attention_mixed = lax.map(jax.checkpoint(attend), (queries, keys, values, labels))
    attention_mixed = both_ways(attention_mixed)
    residual_stream = hidden_features + bfloat_backward(jnp.einsum('crz,zm->crm', attention_mixed, output_projection_matrix, precision=FINEST_PRECISION))
    normalized_mixer_input = low(root_norm(residual_stream, gain_all[D:]))
    gate_up_activations = bfloat_backward(jnp.einsum('mar,rw->maw', normalized_mixer_input, gate_up_matrix, precision=FINEST_PRECISION))
    hidden_state = low(jax.nn.silu(gate_up_activations[..., :FF]) * gate_up_activations[..., FF:])
    return residual_stream + bfloat_backward(jnp.einsum('gvc,cr->gvr', hidden_state, down_projection_matrix, precision=FINEST_PRECISION))

def reference(layer_input, segments, project_weight, output_weight, gate_up_weight, down_weight, gains, cotangent):
    matrices = (project_weight.astype(jnp.float32).reshape(D, (H + 2 * KV) * HD), output_weight.astype(jnp.float32).reshape(H * HD, D), gate_up_weight.astype(jnp.float32).reshape(D, 2 * FF), down_weight.astype(jnp.float32).reshape(FF, D))
    gain_all = gains.astype(jnp.float32)
    group = math.gcd(NSEQ, max(1, 4096 // LEN))
    count = NSEQ // group
    hidden_features = layer_input.astype(jnp.float32).reshape(count, group, LEN, D)
    tangents = cotangent.astype(jnp.float32).reshape(count, group, LEN, D)
    labels = segments.reshape(count, group, LEN)

    def step(carry, item):
        block, tangent, label_block = item

        def forward(block_in, attention_project_matrix, output_projection_matrix, gate_up_matrix, down_projection_matrix, gain_vec):
            return layer(block_in, attention_project_matrix, output_projection_matrix, gate_up_matrix, down_projection_matrix, gain_vec, label_block)
        outcome, pull = jax.vjp(forward, block, *matrices, gain_all)
        deltas = pull(tangent)
        carry = tuple((total + part for total, part in zip(carry, deltas[1:])))
        return (carry, (outcome.astype(jnp.bfloat16), deltas[0].astype(jnp.bfloat16)))
    initial = tuple((jnp.zeros_like(part) for part in matrices + (gain_all,)))
    sums, (results, deltas) = lax.scan(step, initial, (hidden_features, tangents, labels))
    return (results.reshape(NSEQ, LEN, D), deltas.reshape(NSEQ, LEN, D), sums[0].reshape(-1), sums[1].reshape(-1), sums[2].reshape(-1), sums[3].reshape(-1), sums[4])
```

```python
import jax
import jax.numpy as jnp
from jax import lax
from jax.experimental import pallas as pl
from jax.experimental.pallas import tpu as pltpu
from jax.sharding import PartitionSpec as P

D = 576
H = 9
KV = 3
HD = 64
FF = 1536
GROUP = H // KV
ROWS = 128

EPSILON = 1e-05
THETA = 100000.0
MASKED = -1e30
VMEM_LIMIT = 48 * 1024 * 1024


def root_norm(values, gain):
    return values * lax.rsqrt(jnp.mean(values * values, axis=-1, keepdims=True) + EPSILON) * gain


def gated_unit(gate_up_activations):
    middle = gate_up_activations.shape[-1] // 2
    return jax.nn.silu(gate_up_activations[..., :middle]) * gate_up_activations[..., middle:]


def shifted(block, axis, distance):
    devices = range(lax.axis_size(axis))
    route = [(i - distance, i) for i in devices if i - distance in devices]
    return lax.ppermute(block, axis, route)


def halved(block, axis, bit):
    size = lax.axis_size(axis)
    mine = (lax.axis_index(axis) // bit) % 2
    low = block.astype(jnp.bfloat16)
    away = lax.dynamic_index_in_dim(low, 1 - mine, axis=1, keepdims=False)
    kept = lax.dynamic_index_in_dim(block, mine, axis=1, keepdims=False)
    came = lax.ppermute(away, axis, [(i, i ^ bit) for i in range(size)])
    return kept.astype(jnp.float32) + came.astype(jnp.float32)


def reduce_scatter(parts, shards, halves):
    sizes = [part.shape[-1] for part in parts]
    total = sum(sizes)
    padded = -(-total // 128) * 128
    joined = jnp.concatenate([part.astype(jnp.bfloat16) for part in parts], axis=-1)
    joined = jnp.pad(joined, ((0, 0), (0, 0), (0, padded - total)))
    block = joined.reshape(shards, halves, padded // 128, 128)
    block = halved(block, "seq", 1)
    bit = 1
    while bit < shards:
        block = halved(block.reshape(-1, 2, padded // 128, 128), "fsdp", bit)
        bit *= 2
    flat = block.reshape(-1)
    outs, at = [], 0
    for size in sizes:
        outs.append(flat[at : at + size])
        at += size
    return outs


def project_kernel(x_ref, gain_ref, weight_ref, cos_ref, sin_ref, normed_ref, queries_ref, kv_ref):
    x = x_ref[0].astype(jnp.float32)
    normed = root_norm(x, gain_ref[...]).astype(jnp.bfloat16)
    normed_ref[0] = normed
    projected = lax.dot_general(
        weight_ref[...], normed, (((1,), (1,)), ((), ())), preferred_element_type=jnp.float32
    )
    cos = cos_ref[...]
    sin = sin_ref[...]
    keys = []
    for head in range(H + KV):
        first = projected[head * HD : head * HD + 32]
        second = projected[head * HD + 32 : (head + 1) * HD]
        turned = jnp.concatenate([first * cos - second * sin, second * cos + first * sin], axis=0)
        if head < H:
            low = turned.astype(jnp.bfloat16).astype(jnp.float32) * HD ** (-0.5)
            queries_ref[0, head * HD : (head + 1) * HD, :] = low.astype(jnp.bfloat16)
        else:
            keys.append(turned)
    both = jnp.concatenate(keys + [projected[(H + KV) * HD :]], axis=0)
    kv_ref[0] = both.T.astype(jnp.bfloat16)


def project(x, gain, weight_t, cos, sin):
    count, half = x.shape[0], x.shape[1]
    wide = (H + 2 * KV) * HD
    return pl.pallas_call(
        project_kernel,
        grid=(count,),
        in_specs=[
            pl.BlockSpec((1, half, D), lambda i: (i, 0, 0)),
            pl.BlockSpec((1, D), lambda i: (0, 0)),
            pl.BlockSpec((wide, D), lambda i: (0, 0)),
            pl.BlockSpec((32, half), lambda i: (0, 0)),
            pl.BlockSpec((32, half), lambda i: (0, 0)),
        ],
        out_specs=[
            pl.BlockSpec((1, half, D), lambda i: (i, 0, 0)),
            pl.BlockSpec((1, H * HD, half), lambda i: (i, 0, 0)),
            pl.BlockSpec((1, half, 2 * KV * HD), lambda i: (i, 0, 0)),
        ],
        out_shape=[
            jax.ShapeDtypeStruct((count, half, D), jnp.bfloat16),
            jax.ShapeDtypeStruct((count, H * HD, half), jnp.bfloat16),
            jax.ShapeDtypeStruct((count, half, 2 * KV * HD), jnp.bfloat16),
        ],
        compiler_params=pltpu.CompilerParams(vmem_limit_bytes=VMEM_LIMIT),
        cost_estimate=pl.CostEstimate(
            flops=2 * count * half * D * wide, bytes_accessed=count * half * 4096, transcendentals=0
        ),
    )(x, gain, weight_t, cos, sin)


WIDTHS = (1, 2, 3, 4, 5, 6, 8)


def load_window(far_ref, near_ref, labels_ref, keys, values, key_labels):
    half = near_ref.shape[1]
    for group in range(KV):
        at = slice(group * HD, (group + 1) * HD)
        later = slice((KV + group) * HD, (KV + group + 1) * HD)
        keys[group, :half, :] = far_ref[0, :, at]
        keys[group, half:, :] = near_ref[0, :, at]
        values[group, :half, :] = far_ref[0, :, later]
        values[group, half:, :] = near_ref[0, :, later]
    key_labels[...] = jnp.broadcast_to(labels_ref[0], (ROWS, 2 * half)).T


def window_bias(width, start, query_start, labels_ref, key_labels):
    query_row = labels_ref[0, :, pl.ds(query_start, ROWS)]
    same = key_labels[pl.ds(start, width * ROWS), :] == query_row
    shape = (width * ROWS, ROWS)
    key_place = lax.broadcasted_iota(jnp.int32, shape, 0) + start
    query_place = lax.broadcasted_iota(jnp.int32, shape, 1) + query_start
    bias = jnp.where(same & (key_place <= query_place), 0.0, MASKED)
    return jnp.concatenate([bias] * GROUP, axis=1)


def side_by_side(block, group):
    return jnp.concatenate(
        [block[(group * GROUP + i) * HD : (group * GROUP + i + 1) * HD] for i in range(GROUP)], axis=1
    )


def over_widths(first_ref, body):
    block = pl.program_id(1)
    blocks = pl.num_programs(1)
    diagonal = blocks + block
    need = diagonal + 1 - first_ref[pl.program_id(0), block]
    below = 0
    for width in WIDTHS:
        if width > 8:
            continue

        @pl.when((need > below) & (need <= width))
        def _(width=width):
            start = jnp.maximum(diagonal + 1 - width, 0) * ROWS
            body(width, pl.multiple_of(start, ROWS))

        below = width


def forward_kernel(
    first_ref, queries_ref, far_ref, near_ref, labels_ref, mixed_ref, log_ref, keys, values, key_labels, mixed_t
):
    @pl.when(pl.program_id(1) == 0)
    def _():
        load_window(far_ref, near_ref, labels_ref, keys, values, key_labels)

    query_start = pl.multiple_of(near_ref.shape[1] + pl.program_id(1) * ROWS, ROWS)

    def body(width, start):
        bias = window_bias(width, start, query_start, labels_ref, key_labels)
        queries = queries_ref[0]
        window = pl.ds(start, width * ROWS)
        for group in range(KV):
            scores = jnp.dot(
                keys[group, window, :], side_by_side(queries, group), preferred_element_type=jnp.float32
            )
            scores = scores + bias
            top = jnp.max(scores, axis=0, keepdims=True)
            powers = jnp.exp(scores - top)
            total = jnp.sum(powers, axis=0, keepdims=True)
            weights = (powers * (1.0 / total)).astype(jnp.bfloat16)
            out = lax.dot_general(
                values[group, window, :], weights, (((0,), (0,)), ((), ())), preferred_element_type=jnp.float32
            )
            log_ref[0, 0, group : group + 1, :] = top + jnp.log(total)
            for i in range(GROUP):
                head = group * GROUP + i
                mixed_t[head * HD : (head + 1) * HD, :] = out[:, i * ROWS : (i + 1) * ROWS]

    over_widths(first_ref, body)
    mixed_ref[0] = mixed_t[...].T.astype(jnp.bfloat16)


def attention_forward(first, queries, far, near, labels):
    count, half = near.shape[0], near.shape[1]
    blocks = half // ROWS
    wide = 2 * KV * HD
    grid_spec = pltpu.PrefetchScalarGridSpec(
        num_scalar_prefetch=1,
        grid=(count, blocks),
        in_specs=[
            pl.BlockSpec((1, H * HD, ROWS), lambda i, j, s: (i, 0, j)),
            pl.BlockSpec((1, half, wide), lambda i, j, s: (i, 0, 0)),
            pl.BlockSpec((1, half, wide), lambda i, j, s: (i, 0, 0)),
            pl.BlockSpec((1, 1, 2 * half), lambda i, j, s: (i, 0, 0)),
        ],
        out_specs=[
            pl.BlockSpec((1, ROWS, H * HD), lambda i, j, s: (i, j, 0)),
            pl.BlockSpec((1, 1, 8, GROUP * ROWS), lambda i, j, s: (i, j, 0, 0)),
        ],
        scratch_shapes=[
            pltpu.VMEM((KV, 2 * half, HD), jnp.bfloat16),
            pltpu.VMEM((KV, 2 * half, HD), jnp.bfloat16),
            pltpu.VMEM((2 * half, ROWS), jnp.float32),
            pltpu.VMEM((H * HD, ROWS), jnp.float32),
        ],
    )
    return pl.pallas_call(
        forward_kernel,
        grid_spec=grid_spec,
        out_shape=[
            jax.ShapeDtypeStruct((count, half, H * HD), jnp.bfloat16),
            jax.ShapeDtypeStruct((count, blocks, 8, GROUP * ROWS), jnp.float32),
        ],
        compiler_params=pltpu.CompilerParams(vmem_limit_bytes=VMEM_LIMIT),
        cost_estimate=pl.CostEstimate(
            flops=count * H * half * half * HD * 16, bytes_accessed=count * half * 4096, transcendentals=0
        ),
    )(first, queries, far, near, labels)


def backward_kernel(
    first_ref, queries_ref, delta_ref, log_ref, far_ref, near_ref, labels_ref, cos_ref, sin_ref,
    delta_queries_ref, delta_far_ref, delta_near_ref,
    keys, values, key_labels, turned_t, sums,
):
    half = near_ref.shape[1]
    block = pl.program_id(1)

    @pl.when(block == 0)
    def _():
        load_window(far_ref, near_ref, labels_ref, keys, values, key_labels)
        sums[...] = jnp.zeros_like(sums)

    query_start = pl.multiple_of(half + block * ROWS, ROWS)

    def body(width, start):
        bias = window_bias(width, start, query_start, labels_ref, key_labels)
        queries = queries_ref[0]
        deltas = delta_ref[0].astype(jnp.float32).T.astype(jnp.bfloat16)
        window = pl.ds(start, width * ROWS)
        cos = cos_ref[:, pl.ds(query_start, ROWS)]
        sin = sin_ref[:, pl.ds(query_start, ROWS)]
        for group in range(KV):
            key = keys[group, window, :]
            query = side_by_side(queries, group)
            delta = side_by_side(deltas, group)
            scores = jnp.dot(key, query, preferred_element_type=jnp.float32) + bias
            probs = jnp.exp(scores - log_ref[0, 0, group : group + 1, :])
            delta_probs = jnp.dot(values[group, window, :], delta, preferred_element_type=jnp.float32)
            row_dot = jnp.sum(probs * delta_probs, axis=0, keepdims=True)
            delta_scores = (probs * (delta_probs - row_dot)).astype(jnp.bfloat16)
            out = lax.dot_general(
                key, delta_scores, (((0,), (0,)), ((), ())), preferred_element_type=jnp.float32
            ) * HD ** (-0.5)
            sums[group, window, :] += lax.dot_general(
                delta_scores, query, (((1,), (1,)), ((), ())), preferred_element_type=jnp.float32
            )
            sums[KV + group, window, :] += lax.dot_general(
                probs.astype(jnp.bfloat16), delta, (((1,), (1,)), ((), ())), preferred_element_type=jnp.float32
            )
            for i in range(GROUP):
                at = (group * GROUP + i) * HD
                first = out[:32, i * ROWS : (i + 1) * ROWS]
                second = out[32:, i * ROWS : (i + 1) * ROWS]
                turned_t[at : at + 32, :] = first * cos + second * sin
                turned_t[at + 32 : at + HD, :] = second * cos - first * sin

    over_widths(first_ref, body)
    delta_queries_ref[0] = turned_t[...].T.astype(jnp.bfloat16)

    @pl.when(block == pl.num_programs(1) - 1)
    def _():
        pieces = []
        for group in range(KV):
            flipped = sums[group].T
            first, second = flipped[:32], flipped[32:]
            pieces.append(first * cos_ref[...] + second * sin_ref[...])
            pieces.append(second * cos_ref[...] - first * sin_ref[...])
        key_sums = jnp.concatenate(pieces, axis=0).T
        value_sums = jnp.concatenate([sums[KV + group] for group in range(KV)], axis=1)
        wide = KV * HD
        delta_far_ref[0, :, :wide] = key_sums[:half].astype(jnp.bfloat16)
        delta_far_ref[0, :, wide:] = value_sums[:half].astype(jnp.bfloat16)
        delta_near_ref[0, :, :wide] = key_sums[half:]
        delta_near_ref[0, :, wide:] = value_sums[half:]


def attention_backward(first, queries, delta_mixed, logs, far, near, labels, cos, sin):
    count, half = near.shape[0], near.shape[1]
    blocks = half // ROWS
    wide = 2 * KV * HD
    grid_spec = pltpu.PrefetchScalarGridSpec(
        num_scalar_prefetch=1,
        grid=(count, blocks),
        in_specs=[
            pl.BlockSpec((1, H * HD, ROWS), lambda i, j, s: (i, 0, j)),
            pl.BlockSpec((1, ROWS, H * HD), lambda i, j, s: (i, j, 0)),
            pl.BlockSpec((1, 1, 8, GROUP * ROWS), lambda i, j, s: (i, j, 0, 0)),
            pl.BlockSpec((1, half, wide), lambda i, j, s: (i, 0, 0)),
            pl.BlockSpec((1, half, wide), lambda i, j, s: (i, 0, 0)),
            pl.BlockSpec((1, 1, 2 * half), lambda i, j, s: (i, 0, 0)),
            pl.BlockSpec((32, 2 * half), lambda i, j, s: (0, 0)),
            pl.BlockSpec((32, 2 * half), lambda i, j, s: (0, 0)),
        ],
        out_specs=[
            pl.BlockSpec((1, ROWS, H * HD), lambda i, j, s: (i, j, 0)),
            pl.BlockSpec((1, half, wide), lambda i, j, s: (i, 0, 0)),
            pl.BlockSpec((1, half, wide), lambda i, j, s: (i, 0, 0)),
        ],
        scratch_shapes=[
            pltpu.VMEM((KV, 2 * half, HD), jnp.bfloat16),
            pltpu.VMEM((KV, 2 * half, HD), jnp.bfloat16),
            pltpu.VMEM((2 * half, ROWS), jnp.float32),
            pltpu.VMEM((H * HD, ROWS), jnp.float32),
            pltpu.VMEM((2 * KV, 2 * half, HD), jnp.float32),
        ],
    )
    return pl.pallas_call(
        backward_kernel,
        grid_spec=grid_spec,
        out_shape=[
            jax.ShapeDtypeStruct((count, half, H * HD), jnp.bfloat16),
            jax.ShapeDtypeStruct((count, half, wide), jnp.bfloat16),
            jax.ShapeDtypeStruct((count, half, wide), jnp.float32),
        ],
        compiler_params=pltpu.CompilerParams(vmem_limit_bytes=VMEM_LIMIT),
        cost_estimate=pl.CostEstimate(
            flops=count * H * half * half * HD * 40, bytes_accessed=count * half * 8192, transcendentals=0
        ),
    )(first, queries, delta_mixed, logs, far, near, labels, cos, sin)


def per_device(
    layer_input,
    segments,
    project_weight,
    output_weight,
    gate_up_weight,
    down_weight,
    gains,
    cotangent,
):
    sequences, half = layer_input.shape[0], layer_input.shape[1]
    shards, halves = lax.axis_size("fsdp"), lax.axis_size("seq")
    both = ("fsdp", "seq")

    cut, own = project_weight.shape[0], gains.shape[0]
    fill = jnp.zeros((-(cut + own) % 128,), gains.dtype)
    early = lax.all_gather(jnp.concatenate([project_weight, gains, fill]), both, axis=0, tiled=True)
    early = early.reshape(shards * halves, -1)
    project_matrix = early[:, :cut].reshape(D, (H + 2 * KV) * HD)
    gain_whole = early[::halves, cut : cut + own].reshape(2 * D).astype(jnp.float32)
    output_matrix = lax.all_gather(output_weight, both, axis=0, tiled=True).reshape(H * HD, D)
    gate_up_matrix = lax.all_gather(gate_up_weight, both, axis=0, tiled=True).reshape(D, 2 * FF)
    down_matrix = lax.all_gather(down_weight, both, axis=0, tiled=True).reshape(FF, D)

    start = lax.axis_index("seq") * half
    places = start - half + jnp.arange(2 * half, dtype=jnp.int32)
    rates = THETA ** (-(jnp.arange(HD // 2, dtype=jnp.float32) * 2.0) / HD)
    angle = rates[:, None] * places.astype(jnp.float32)[None, :]
    cos, sin = jnp.cos(angle), jnp.sin(angle)
    padded = jnp.concatenate([jnp.full((sequences, half), -1, jnp.int32), segments], axis=1)
    key_labels = lax.dynamic_slice_in_dim(padded, start, 2 * half, axis=1)
    block_labels = key_labels[:, half::ROWS]
    first = (
        jnp.sum((key_labels[:, None, :] < block_labels[:, :, None]).astype(jnp.int32), axis=-1) // ROWS
    )
    labels = key_labels.astype(jnp.float32)[:, None, :]

    normed, queries, near = project(
        layer_input, gain_whole[None, :D], project_matrix.T, cos[:, half:], sin[:, half:]
    )
    far = shifted(near, "seq", 1)
    mixed, logs = attention_forward(first, queries, far, near, labels)

    hidden_features = layer_input.astype(jnp.float32)
    residual_stream = hidden_features + jnp.einsum(
        "crz,zm->crm", mixed, output_matrix, preferred_element_type=jnp.float32
    )
    mixer_input = root_norm(residual_stream, gain_whole[D:]).astype(jnp.bfloat16)
    gate_up_activations = jnp.einsum(
        "mar,rw->maw", mixer_input, gate_up_matrix, preferred_element_type=jnp.float32
    )
    hidden_state, unit_pull = jax.vjp(gated_unit, gate_up_activations)
    hidden_low = hidden_state.astype(jnp.bfloat16)
    result = (
        residual_stream
        + jnp.einsum("gvc,cr->gvr", hidden_low, down_matrix, preferred_element_type=jnp.float32)
    ).astype(jnp.bfloat16)
    delta_down = jnp.einsum(
        "rqh,rqo->ho", hidden_low, cotangent, preferred_element_type=jnp.float32
    )
    delta_hidden = jnp.einsum(
        "iou,eu->ioe", cotangent, down_matrix, preferred_element_type=jnp.float32
    )
    gate_up_cotangent = unit_pull(delta_hidden)[0].astype(jnp.bfloat16)
    delta_gate_up = jnp.einsum(
        "bqg,bqv->gv", mixer_input, gate_up_cotangent, preferred_element_type=jnp.float32
    )
    delta_mixer = jnp.einsum(
        "evi,ai->eva", gate_up_cotangent, gate_up_matrix, preferred_element_type=jnp.float32
    )
    mixer_pull = jax.vjp(root_norm, residual_stream, gain_whole[D:])[1]
    delta_residual, delta_gain_mixer = mixer_pull(delta_mixer)
    delta_residual = delta_residual + cotangent.astype(jnp.float32)
    branch = delta_residual.astype(jnp.bfloat16)
    delta_output = jnp.einsum("zxa,zxq->aq", mixed, branch, preferred_element_type=jnp.float32)
    delta_mixed = jnp.einsum(
        "wrc,jc->wrj", branch, output_matrix, preferred_element_type=jnp.float32
    ).astype(jnp.bfloat16)

    def spread(matrix):
        return matrix.astype(jnp.bfloat16).reshape(shards, halves, -1)

    gate_up_gradient, down_gradient, output_gradient = reduce_scatter(
        [spread(delta_gate_up), spread(delta_down), spread(delta_output)], shards, halves
    )

    pieces = []
    for i in range(sequences):
        at = slice(i, i + 1)
        pieces.append(
            attention_backward(
                first[at], queries[at], delta_mixed[at], logs[at], far[at], near[at], labels[at], cos, sin
            )
        )
    delta_queries, delta_far, delta_near = [jnp.concatenate(piece, axis=0) for piece in zip(*pieces)]
    back = shifted(delta_far, "seq", -1)
    delta_kv = (delta_near + back.astype(jnp.float32)).astype(jnp.bfloat16)
    projected_cotangent = jnp.concatenate([delta_queries, delta_kv], axis=-1)
    delta_project = jnp.einsum(
        "zgv,zgf->vf", normed, projected_cotangent, preferred_element_type=jnp.float32
    )
    delta_normed = jnp.einsum(
        "xgc,fc->xgf", projected_cotangent, project_matrix, preferred_element_type=jnp.float32
    )
    attend_pull = jax.vjp(root_norm, hidden_features, gain_whole[:D])[1]
    delta_features, delta_gain_attend = attend_pull(delta_normed)
    input_gradient = (delta_residual + delta_features).astype(jnp.bfloat16)
    delta_gain = jnp.concatenate([delta_gain_attend, delta_gain_mixer]).reshape(shards, 1, -1)
    project_gradient, gains_gradient = reduce_scatter(
        [spread(delta_project), jnp.broadcast_to(delta_gain, (shards, halves, delta_gain.shape[-1]))],
        shards,
        halves,
    )
    return (
        result,
        input_gradient,
        project_gradient,
        output_gradient,
        gate_up_gradient,
        down_gradient,
        gains_gradient,
    )


def solution(mesh):
    return jax.shard_map(
        per_device,
        mesh=mesh,
        in_specs=(
            P("fsdp", "seq", None),
            P("fsdp", None),
            P(("fsdp", "seq")),
            P(("fsdp", "seq")),
            P(("fsdp", "seq")),
            P(("fsdp", "seq")),
            P("fsdp"),
            P("fsdp", "seq", None),
        ),
        out_specs=(
            P("fsdp", "seq", None),
            P("fsdp", "seq", None),
            P(("fsdp", "seq")),
            P(("fsdp", "seq")),
            P(("fsdp", "seq")),
            P(("fsdp", "seq")),
            P("fsdp"),
        ),
        check_vma=False,
    )
```

```python
import jax
import jax.numpy as jnp
from jax import lax
from jax.experimental import pallas as pl
from jax.experimental.pallas import tpu as pltpu
from jax.sharding import PartitionSpec as P

D = 576
H = 9
KV = 3
HD = 64
FF = 1536
GROUP = H // KV
ROWS = 128

EPSILON = 1e-05
THETA = 100000.0
MASKED = -1e30
VMEM_LIMIT = 48 * 1024 * 1024


def root_norm(values, gain):
    return values * lax.rsqrt(jnp.mean(values * values, axis=-1, keepdims=True) + EPSILON) * gain


def gated_unit(gate_up_activations):
    middle = gate_up_activations.shape[-1] // 2
    return jax.nn.silu(gate_up_activations[..., :middle]) * gate_up_activations[..., middle:]


def shifted(block, axis, distance):
    devices = range(lax.axis_size(axis))
    route = [(i - distance, i) for i in devices if i - distance in devices]
    return lax.ppermute(block, axis, route)


def away_and_kept(block, axis, bit, place):
    mine = (lax.axis_index(axis) // bit) % 2
    parted = block.reshape((-1, 2, place) + block.shape[1:])
    tail = block.shape[1:]
    away = lax.dynamic_index_in_dim(parted, 1 - mine, axis=1, keepdims=False).reshape((-1,) + tail)
    kept = lax.dynamic_index_in_dim(parted, mine, axis=1, keepdims=False).reshape((-1,) + tail)
    return away.astype(jnp.bfloat16), kept


def exchanged(away, axis, bit):
    return lax.ppermute(away, axis, [(i, i ^ bit) for i in range(lax.axis_size(axis))])


def steps_of(shards, swapped):
    bits = []
    while 2 ** len(bits) < shards:
        bits.append(2 ** len(bits))
    steps = [("seq", 1, 1)]
    if swapped and len(bits) > 1:
        steps += [("fsdp", 2, 2), ("fsdp", 1, 1)]
        bits = bits[2:]
    return steps + [("fsdp", bit, 1) for bit in bits]


def joined_parts(parts):
    total = sum(part.shape[-1] for part in parts)
    joined = jnp.concatenate([part.astype(jnp.bfloat16) for part in parts], axis=-1)
    joined = jnp.pad(joined, ((0, 0), (0, 0), (0, -total % 128)))
    return joined.reshape(joined.shape[0] * joined.shape[1], -1, 128)


def cut_apart(block, parts):
    flat = block.reshape(-1)
    outs, at = [], 0
    for part in parts:
        outs.append(flat[at : at + part.shape[-1]])
        at += part.shape[-1]
    return outs


def added(kept, came):
    return kept.astype(jnp.float32) + came.astype(jnp.float32)


def reduce_scatter(parts, shards):
    block = joined_parts(parts)
    for axis, bit, place in steps_of(shards, False):
        away, kept = away_and_kept(block, axis, bit, place)
        block = added(kept, exchanged(away, axis, bit))
    return cut_apart(block, parts)


def project_kernel(x_ref, gain_ref, weight_ref, cos_ref, sin_ref, normed_ref, queries_ref, kv_ref):
    x = x_ref[0].astype(jnp.float32)
    normed = root_norm(x, gain_ref[...]).astype(jnp.bfloat16)
    normed_ref[0] = normed
    projected = lax.dot_general(
        weight_ref[...], normed, (((1,), (1,)), ((), ())), preferred_element_type=jnp.float32
    )
    cos = cos_ref[...]
    sin = sin_ref[...]
    keys = []
    for head in range(H + KV):
        first = projected[head * HD : head * HD + 32]
        second = projected[head * HD + 32 : (head + 1) * HD]
        turned = jnp.concatenate([first * cos - second * sin, second * cos + first * sin], axis=0)
        if head < H:
            low = turned.astype(jnp.bfloat16).astype(jnp.float32) * HD ** (-0.5)
            queries_ref[0, head * HD : (head + 1) * HD, :] = low.astype(jnp.bfloat16)
        else:
            keys.append(turned)
    both = jnp.concatenate(keys + [projected[(H + KV) * HD :]], axis=0)
    kv_ref[0] = both.T.astype(jnp.bfloat16)


def project(x, gain, weight_t, cos, sin):
    count, half = x.shape[0], x.shape[1]
    wide = (H + 2 * KV) * HD
    return pl.pallas_call(
        project_kernel,
        grid=(count,),
        in_specs=[
            pl.BlockSpec((1, half, D), lambda i: (i, 0, 0)),
            pl.BlockSpec((1, D), lambda i: (0, 0)),
            pl.BlockSpec((wide, D), lambda i: (0, 0)),
            pl.BlockSpec((32, half), lambda i: (0, 0)),
            pl.BlockSpec((32, half), lambda i: (0, 0)),
        ],
        out_specs=[
            pl.BlockSpec((1, half, D), lambda i: (i, 0, 0)),
            pl.BlockSpec((1, H * HD, half), lambda i: (i, 0, 0)),
            pl.BlockSpec((1, half, 2 * KV * HD), lambda i: (i, 0, 0)),
        ],
        out_shape=[
            jax.ShapeDtypeStruct((count, half, D), jnp.bfloat16),
            jax.ShapeDtypeStruct((count, H * HD, half), jnp.bfloat16),
            jax.ShapeDtypeStruct((count, half, 2 * KV * HD), jnp.bfloat16),
        ],
        compiler_params=pltpu.CompilerParams(vmem_limit_bytes=VMEM_LIMIT),
        cost_estimate=pl.CostEstimate(
            flops=2 * count * half * D * wide, bytes_accessed=count * half * 4096, transcendentals=0
        ),
    )(x, gain, weight_t, cos, sin)


WIDTHS = (1, 2, 3, 4, 5, 6, 8)


def load_window(far_ref, near_ref, labels_ref, keys, values, key_labels):
    half = near_ref.shape[1]
    for group in range(KV):
        at = slice(group * HD, (group + 1) * HD)
        later = slice((KV + group) * HD, (KV + group + 1) * HD)
        keys[group, :half, :] = far_ref[0, :, at]
        keys[group, half:, :] = near_ref[0, :, at]
        values[group, :half, :] = far_ref[0, :, later]
        values[group, half:, :] = near_ref[0, :, later]
    key_labels[...] = jnp.broadcast_to(labels_ref[0], (ROWS, 2 * half)).T


def window_bias(width, start, query_start, labels_ref, key_labels):
    query_row = labels_ref[0, :, pl.ds(query_start, ROWS)]
    same = key_labels[pl.ds(start, width * ROWS), :] == query_row
    shape = (width * ROWS, ROWS)
    key_place = lax.broadcasted_iota(jnp.int32, shape, 0) + start
    query_place = lax.broadcasted_iota(jnp.int32, shape, 1) + query_start
    bias = jnp.where(same & (key_place <= query_place), 0.0, MASKED)
    return jnp.concatenate([bias] * GROUP, axis=1)


def side_by_side(block, group):
    return jnp.concatenate(
        [block[(group * GROUP + i) * HD : (group * GROUP + i + 1) * HD] for i in range(GROUP)], axis=1
    )


def over_widths(first_ref, body):
    block = pl.program_id(1)
    blocks = pl.num_programs(1)
    diagonal = blocks + block
    need = diagonal + 1 - first_ref[pl.program_id(0), block]
    below = 0
    for width in WIDTHS:
        if width > 8:
            continue

        @pl.when((need > below) & (need <= width))
        def _(width=width):
            start = jnp.maximum(diagonal + 1 - width, 0) * ROWS
            body(width, pl.multiple_of(start, ROWS))

        below = width


def forward_kernel(
    first_ref, queries_ref, far_ref, near_ref, labels_ref, mixed_ref, log_ref, keys, values, key_labels, mixed_t
):
    @pl.when(pl.program_id(1) == 0)
    def _():
        load_window(far_ref, near_ref, labels_ref, keys, values, key_labels)

    query_start = pl.multiple_of(near_ref.shape[1] + pl.program_id(1) * ROWS, ROWS)

    def body(width, start):
        bias = window_bias(width, start, query_start, labels_ref, key_labels)
        queries = queries_ref[0]
        window = pl.ds(start, width * ROWS)
        for group in range(KV):
            scores = jnp.dot(
                keys[group, window, :], side_by_side(queries, group), preferred_element_type=jnp.float32
            )
            scores = scores + bias
            top = jnp.max(scores, axis=0, keepdims=True)
            powers = jnp.exp(scores - top)
            total = jnp.sum(powers, axis=0, keepdims=True)
            weights = (powers * (1.0 / total)).astype(jnp.bfloat16)
            out = lax.dot_general(
                values[group, window, :], weights, (((0,), (0,)), ((), ())), preferred_element_type=jnp.float32
            )
            log_ref[0, 0, group : group + 1, :] = top + jnp.log(total)
            for i in range(GROUP):
                head = group * GROUP + i
                mixed_t[head * HD : (head + 1) * HD, :] = out[:, i * ROWS : (i + 1) * ROWS]

    over_widths(first_ref, body)
    mixed_ref[0] = mixed_t[...].T.astype(jnp.bfloat16)


def attention_forward(first, queries, far, near, labels):
    count, half = near.shape[0], near.shape[1]
    blocks = half // ROWS
    wide = 2 * KV * HD
    grid_spec = pltpu.PrefetchScalarGridSpec(
        num_scalar_prefetch=1,
        grid=(count, blocks),
        in_specs=[
            pl.BlockSpec((1, H * HD, ROWS), lambda i, j, s: (i, 0, j)),
            pl.BlockSpec((1, half, wide), lambda i, j, s: (i, 0, 0)),
            pl.BlockSpec((1, half, wide), lambda i, j, s: (i, 0, 0)),
            pl.BlockSpec((1, 1, 2 * half), lambda i, j, s: (i, 0, 0)),
        ],
        out_specs=[
            pl.BlockSpec((1, ROWS, H * HD), lambda i, j, s: (i, j, 0)),
            pl.BlockSpec((1, 1, 8, GROUP * ROWS), lambda i, j, s: (i, j, 0, 0)),
        ],
        scratch_shapes=[
            pltpu.VMEM((KV, 2 * half, HD), jnp.bfloat16),
            pltpu.VMEM((KV, 2 * half, HD), jnp.bfloat16),
            pltpu.VMEM((2 * half, ROWS), jnp.float32),
            pltpu.VMEM((H * HD, ROWS), jnp.float32),
        ],
    )
    return pl.pallas_call(
        forward_kernel,
        grid_spec=grid_spec,
        out_shape=[
            jax.ShapeDtypeStruct((count, half, H * HD), jnp.bfloat16),
            jax.ShapeDtypeStruct((count, blocks, 8, GROUP * ROWS), jnp.float32),
        ],
        compiler_params=pltpu.CompilerParams(vmem_limit_bytes=VMEM_LIMIT),
        cost_estimate=pl.CostEstimate(
            flops=count * H * half * half * HD * 16, bytes_accessed=count * half * 4096, transcendentals=0
        ),
    )(first, queries, far, near, labels)


def backward_kernel(
    first_ref, queries_ref, delta_ref, log_ref, far_ref, near_ref, labels_ref, cos_ref, sin_ref,
    delta_queries_ref, delta_far_ref, delta_near_ref,
    keys, values, key_labels, turned_t, sums,
):
    half = near_ref.shape[1]
    block = pl.program_id(1)

    @pl.when(block == 0)
    def _():
        load_window(far_ref, near_ref, labels_ref, keys, values, key_labels)
        sums[...] = jnp.zeros_like(sums)

    query_start = pl.multiple_of(half + block * ROWS, ROWS)

    def body(width, start):
        bias = window_bias(width, start, query_start, labels_ref, key_labels)
        queries = queries_ref[0]
        deltas = delta_ref[0].astype(jnp.float32).T.astype(jnp.bfloat16)
        window = pl.ds(start, width * ROWS)
        cos = cos_ref[:, pl.ds(query_start, ROWS)]
        sin = sin_ref[:, pl.ds(query_start, ROWS)]
        for group in range(KV):
            key = keys[group, window, :]
            query = side_by_side(queries, group)
            delta = side_by_side(deltas, group)
            scores = jnp.dot(key, query, preferred_element_type=jnp.float32) + bias
            probs = jnp.exp(scores - log_ref[0, 0, group : group + 1, :])
            delta_probs = jnp.dot(values[group, window, :], delta, preferred_element_type=jnp.float32)
            row_dot = jnp.sum(probs * delta_probs, axis=0, keepdims=True)
            delta_scores = (probs * (delta_probs - row_dot)).astype(jnp.bfloat16)
            out = lax.dot_general(
                key, delta_scores, (((0,), (0,)), ((), ())), preferred_element_type=jnp.float32
            ) * HD ** (-0.5)
            sums[group, window, :] += lax.dot_general(
                delta_scores, query, (((1,), (1,)), ((), ())), preferred_element_type=jnp.float32
            )
            sums[KV + group, window, :] += lax.dot_general(
                probs.astype(jnp.bfloat16), delta, (((1,), (1,)), ((), ())), preferred_element_type=jnp.float32
            )
            for i in range(GROUP):
                at = (group * GROUP + i) * HD
                first = out[:32, i * ROWS : (i + 1) * ROWS]
                second = out[32:, i * ROWS : (i + 1) * ROWS]
                turned_t[at : at + 32, :] = first * cos + second * sin
                turned_t[at + 32 : at + HD, :] = second * cos - first * sin

    over_widths(first_ref, body)
    delta_queries_ref[0] = turned_t[...].T.astype(jnp.bfloat16)

    @pl.when(block == pl.num_programs(1) - 1)
    def _():
        pieces = []
        for group in range(KV):
            flipped = sums[group].T
            first, second = flipped[:32], flipped[32:]
            pieces.append(first * cos_ref[...] + second * sin_ref[...])
            pieces.append(second * cos_ref[...] - first * sin_ref[...])
        key_sums = jnp.concatenate(pieces, axis=0).T
        value_sums = jnp.concatenate([sums[KV + group] for group in range(KV)], axis=1)
        wide = KV * HD
        delta_far_ref[0, :, :wide] = key_sums[:half].astype(jnp.bfloat16)
        delta_far_ref[0, :, wide:] = value_sums[:half].astype(jnp.bfloat16)
        delta_near_ref[0, :, :wide] = key_sums[half:]
        delta_near_ref[0, :, wide:] = value_sums[half:]


def attention_backward(first, queries, delta_mixed, logs, far, near, labels, cos, sin):
    count, half = near.shape[0], near.shape[1]
    blocks = half // ROWS
    wide = 2 * KV * HD
    grid_spec = pltpu.PrefetchScalarGridSpec(
        num_scalar_prefetch=1,
        grid=(count, blocks),
        in_specs=[
            pl.BlockSpec((1, H * HD, ROWS), lambda i, j, s: (i, 0, j)),
            pl.BlockSpec((1, ROWS, H * HD), lambda i, j, s: (i, j, 0)),
            pl.BlockSpec((1, 1, 8, GROUP * ROWS), lambda i, j, s: (i, j, 0, 0)),
            pl.BlockSpec((1, half, wide), lambda i, j, s: (i, 0, 0)),
            pl.BlockSpec((1, half, wide), lambda i, j, s: (i, 0, 0)),
            pl.BlockSpec((1, 1, 2 * half), lambda i, j, s: (i, 0, 0)),
            pl.BlockSpec((32, 2 * half), lambda i, j, s: (0, 0)),
            pl.BlockSpec((32, 2 * half), lambda i, j, s: (0, 0)),
        ],
        out_specs=[
            pl.BlockSpec((1, ROWS, H * HD), lambda i, j, s: (i, j, 0)),
            pl.BlockSpec((1, half, wide), lambda i, j, s: (i, 0, 0)),
            pl.BlockSpec((1, half, wide), lambda i, j, s: (i, 0, 0)),
        ],
        scratch_shapes=[
            pltpu.VMEM((KV, 2 * half, HD), jnp.bfloat16),
            pltpu.VMEM((KV, 2 * half, HD), jnp.bfloat16),
            pltpu.VMEM((2 * half, ROWS), jnp.float32),
            pltpu.VMEM((H * HD, ROWS), jnp.float32),
            pltpu.VMEM((2 * KV, 2 * half, HD), jnp.float32),
        ],
    )
    return pl.pallas_call(
        backward_kernel,
        grid_spec=grid_spec,
        out_shape=[
            jax.ShapeDtypeStruct((count, half, H * HD), jnp.bfloat16),
            jax.ShapeDtypeStruct((count, half, wide), jnp.bfloat16),
            jax.ShapeDtypeStruct((count, half, wide), jnp.float32),
        ],
        compiler_params=pltpu.CompilerParams(vmem_limit_bytes=VMEM_LIMIT),
        cost_estimate=pl.CostEstimate(
            flops=count * H * half * half * HD * 40, bytes_accessed=count * half * 8192, transcendentals=0
        ),
    )(first, queries, delta_mixed, logs, far, near, labels, cos, sin)


def per_device(
    layer_input,
    segments,
    project_weight,
    output_weight,
    gate_up_weight,
    down_weight,
    gains,
    cotangent,
):
    sequences, half = layer_input.shape[0], layer_input.shape[1]
    shards, halves = lax.axis_size("fsdp"), lax.axis_size("seq")
    both = ("fsdp", "seq")

    cut, own = project_weight.shape[0], gains.shape[0]
    fill = jnp.zeros((-(cut + own) % 128,), gains.dtype)
    early = lax.all_gather(jnp.concatenate([project_weight, gains, fill]), both, axis=0, tiled=True)
    early = early.reshape(shards * halves, -1)
    project_matrix = early[:, :cut].reshape(D, (H + 2 * KV) * HD)
    gain_whole = early[::halves, cut : cut + own].reshape(2 * D).astype(jnp.float32)
    output_matrix = lax.all_gather(output_weight, both, axis=0, tiled=True).reshape(H * HD, D)
    gate_up_matrix = lax.all_gather(gate_up_weight, both, axis=0, tiled=True).reshape(D, 2 * FF)
    down_matrix = lax.all_gather(down_weight, both, axis=0, tiled=True).reshape(FF, D)

    start = lax.axis_index("seq") * half
    places = start - half + jnp.arange(2 * half, dtype=jnp.int32)
    rates = THETA ** (-(jnp.arange(HD // 2, dtype=jnp.float32) * 2.0) / HD)
    angle = rates[:, None] * places.astype(jnp.float32)[None, :]
    cos, sin = jnp.cos(angle), jnp.sin(angle)
    padded = jnp.concatenate([jnp.full((sequences, half), -1, jnp.int32), segments], axis=1)
    key_labels = lax.dynamic_slice_in_dim(padded, start, 2 * half, axis=1)
    block_labels = key_labels[:, half::ROWS]
    first = (
        jnp.sum((key_labels[:, None, :] < block_labels[:, :, None]).astype(jnp.int32), axis=-1) // ROWS
    )
    labels = key_labels.astype(jnp.float32)[:, None, :]

    normed, queries, near = project(
        layer_input, gain_whole[None, :D], project_matrix.T, cos[:, half:], sin[:, half:]
    )
    far = shifted(near, "seq", 1)
    mixed, logs = attention_forward(first, queries, far, near, labels)

    hidden_features = layer_input.astype(jnp.float32)
    residual_stream = hidden_features + jnp.einsum(
        "crz,zm->crm", mixed, output_matrix, preferred_element_type=jnp.float32
    )
    mixer_input = root_norm(residual_stream, gain_whole[D:]).astype(jnp.bfloat16)
    gate_up_activations = jnp.einsum(
        "mar,rw->maw", mixer_input, gate_up_matrix, preferred_element_type=jnp.float32
    )
    hidden_state, unit_pull = jax.vjp(gated_unit, gate_up_activations)
    hidden_low = hidden_state.astype(jnp.bfloat16)
    result = (
        residual_stream
        + jnp.einsum("gvc,cr->gvr", hidden_low, down_matrix, preferred_element_type=jnp.float32)
    ).astype(jnp.bfloat16)
    delta_down = jnp.einsum(
        "rqh,rqo->ho", hidden_low, cotangent, preferred_element_type=jnp.float32
    )
    delta_hidden = jnp.einsum(
        "iou,eu->ioe", cotangent, down_matrix, preferred_element_type=jnp.float32
    )
    gate_up_cotangent = unit_pull(delta_hidden)[0].astype(jnp.bfloat16)
    delta_gate_up = jnp.einsum(
        "bqg,bqv->gv", mixer_input, gate_up_cotangent, preferred_element_type=jnp.float32
    )
    delta_mixer = jnp.einsum(
        "evi,ai->eva", gate_up_cotangent, gate_up_matrix, preferred_element_type=jnp.float32
    )
    mixer_pull = jax.vjp(root_norm, residual_stream, gain_whole[D:])[1]
    delta_residual, delta_gain_mixer = mixer_pull(delta_mixer)
    delta_residual = delta_residual + cotangent.astype(jnp.float32)
    branch = delta_residual.astype(jnp.bfloat16)
    delta_output = jnp.einsum("zxa,zxq->aq", mixed, branch, preferred_element_type=jnp.float32)
    delta_mixed = jnp.einsum(
        "wrc,jc->wrj", branch, output_matrix, preferred_element_type=jnp.float32
    ).astype(jnp.bfloat16)

    def spread(matrix):
        return matrix.astype(jnp.bfloat16).reshape(shards, halves, -1)

    wholes = [[spread(delta_gate_up)], [spread(delta_down), spread(delta_output)]]
    routes = [steps_of(shards, False), steps_of(shards, True)]
    blocks = [joined_parts(parts) for parts in wholes]
    pieces, step, pending = [], 0, None
    for i in range(sequences):
        if pending is None and step < len(routes[0]):
            pending = [away_and_kept(block, *route[step]) for block, route in zip(blocks, routes)]
            aways = [away for away, kept in pending]
            delta_mixed, *aways = lax.optimization_barrier([delta_mixed] + aways)
            came = [exchanged(away, *route[step][:2]) for away, route in zip(aways, routes)]
        at = slice(i, i + 1)
        piece = attention_backward(
            first[at], queries[at], delta_mixed[at], logs[at], far[at], near[at], labels[at], cos, sin
        )
        if pending is not None and (step != 1 or i >= 2):
            *piece, came_one, came_two = lax.optimization_barrier(list(piece) + came)
            blocks = [added(kept, new) for (_, kept), new in zip(pending, (came_one, came_two))]
            delta_mixed, *blocks = lax.optimization_barrier([delta_mixed] + blocks)
            pending, step = None, step + 1
        pieces.append(piece)
    if pending is not None:
        blocks = [added(kept, new) for (_, kept), new in zip(pending, came)]
        step += 1
    while step < len(routes[0]):
        for which, route in enumerate(routes):
            away, kept = away_and_kept(blocks[which], *route[step])
            blocks[which] = added(kept, exchanged(away, *route[step][:2]))
        step += 1
    (gate_up_gradient,) = cut_apart(blocks[0], wholes[0])
    down_gradient, output_gradient = cut_apart(blocks[1], wholes[1])

    delta_queries, delta_far, delta_near = [jnp.concatenate(piece, axis=0) for piece in zip(*pieces)]
    back = shifted(delta_far, "seq", -1)
    delta_kv = (delta_near + back.astype(jnp.float32)).astype(jnp.bfloat16)
    projected_cotangent = jnp.concatenate([delta_queries, delta_kv], axis=-1)
    delta_project = jnp.einsum(
        "zgv,zgf->vf", normed, projected_cotangent, preferred_element_type=jnp.float32
    )
    delta_normed = jnp.einsum(
        "xgc,fc->xgf", projected_cotangent, project_matrix, preferred_element_type=jnp.float32
    )
    attend_pull = jax.vjp(root_norm, hidden_features, gain_whole[:D])[1]
    delta_features, delta_gain_attend = attend_pull(delta_normed)
    input_gradient = (delta_residual + delta_features).astype(jnp.bfloat16)
    delta_gain = jnp.concatenate([delta_gain_attend, delta_gain_mixer]).reshape(shards, 1, -1)
    project_gradient, gains_gradient = reduce_scatter(
        [spread(delta_project), jnp.broadcast_to(delta_gain, (shards, halves, delta_gain.shape[-1]))],
        shards,
    )
    return (
        result,
        input_gradient,
        project_gradient,
        output_gradient,
        gate_up_gradient,
        down_gradient,
        gains_gradient,
    )


def solution(mesh):
    return jax.shard_map(
        per_device,
        mesh=mesh,
        in_specs=(
            P("fsdp", "seq", None),
            P("fsdp", None),
            P(("fsdp", "seq")),
            P(("fsdp", "seq")),
            P(("fsdp", "seq")),
            P(("fsdp", "seq")),
            P("fsdp"),
            P("fsdp", "seq", None),
        ),
        out_specs=(
            P("fsdp", "seq", None),
            P("fsdp", "seq", None),
            P(("fsdp", "seq")),
            P(("fsdp", "seq")),
            P(("fsdp", "seq")),
            P(("fsdp", "seq")),
            P("fsdp"),
        ),
        check_vma=False,
    )
```
